32 devices in a mesh: tm: 4 (over y, x), space: 8 (over z, core).
Axes of the slice: x: 2, y: 2, z: 4, core: 2. Of those that a mesh axis runs over, the one named last changes fastest.
Arguments:
- source: float32 [64, 3, 32, 8, 128], P('tm', None, 'space'), may hold values from -24 to 24
- coarse_start: float32 [4, 3, 32, 8, 128], P('tm', None, 'space'), may hold values from -6 to 6
- region: int32 [32, 8, 128], P('space'), may hold values from 0 to 7
- reluctivity: float32 [8], replicated, may hold values from 0.25 to 2
- conductance: float32 [8], replicated, may hold values from 0.25 to 4
Outputs:
- states: float32 [64, 3, 32, 8, 128], P('tm', None, 'space')
The draws below stay inside these ranges and needn't reach their ends.
All inputs are finite; a program needn't handle non-finite values.
Results may differ from the reference program's by a relative error of at most 0.00002.
Values sent between devices are 32-bit elements; how exact they have to be, the bound alone decides.
A program may use at most 64 MiB of HBM per device.

```python
import math
import jax
import jax.numpy as jnp
from jax import lax

NX = 8
NY = 128
COMP = 3
FINE = 16
SWEEPS = 4
REGIONS = 8
COARSE = 4
STEPS = 64
NZ = 32


def plant(array, rng, smallest, top_value):
    extent = array.shape
    index_at = [jax.random.randint(jax.random.fold_in(rng, axis), (), 0, extent[axis]) for axis in range(len(extent))]
    array = array.at[tuple(index_at)].set(smallest)
    longest = extent.index(max(extent))
    index_at[longest] = (index_at[longest] + 1) % extent[longest]
    return array.at[tuple(index_at)].set(top_value)


def block_scale(own_key, extent, pieces, least, top_value):
    def one(dim, blocks):
        heights = jax.random.uniform(jax.random.fold_in(jax.random.fold_in(own_key, 6), dim), (blocks,), jnp.float32, least / len(pieces), top_value / len(pieces))
        return jnp.repeat(jnp.exp(heights), extent[dim] // blocks).reshape((-1,) + (1,) * (len(extent) - dim - 1))

    loudness = one(*pieces[0])
    for cut in pieces[1:]:
        loudness = loudness * one(*cut)
    return loudness


def gaussian(key, dims, spread, reach, pieces=(), kind=jnp.bfloat16):
    values = spread * jax.random.normal(key, dims, jnp.float32)
    if pieces:
        values = values * block_scale(key, dims, pieces, -0.22, 0.18)
    return jnp.clip(values, -reach, reach).astype(kind)


def setup_inputs(seed: int = 0) -> dict:
    keys = jax.random.split(jax.random.key(seed), 6)
    source = gaussian(keys[0], (STEPS, COMP, NZ, NX, NY), 4.0, 24.0, ((0, 4), (2, 8)), jnp.float32)
    coarse_start = gaussian(keys[1], (COARSE, COMP, NZ, NX, NY), 1.0, 6.0, ((0, 4), (2, 8)), jnp.float32)
    region = plant(jax.random.randint(keys[2], (NZ, NX, NY), 0, REGIONS), jax.random.fold_in(keys[2], 1), 0, REGIONS - 1).astype(jnp.int32)
    reluctivity = jnp.clip(jnp.exp(jax.random.uniform(keys[3], (REGIONS,), jnp.float32, math.log(0.25), math.log(2.0))), 0.25, 2.0)
    conductance = jnp.clip(jnp.exp(jax.random.uniform(keys[4], (REGIONS,), jnp.float32, math.log(0.25), math.log(4.0))), 0.25, 4.0)
    return {"source": source, "coarse_start": coarse_start, "region": region, "reluctivity": reluctivity, "conductance": conductance}


lamination_ratio = 8.0


def lookup(region, values_table):
    levels = jnp.arange(values_table.shape[0], dtype=jnp.int32)
    matches = (region[None] == levels[:, None, None, None]).astype(values_table.dtype)
    return jnp.sum(matches * values_table[:, None, None, None], axis=0)


def face_terms(reluct):
    padded = jnp.pad(reluct, ((1, 1), (0, 0), (0, 0)))
    faces_z = (0.5 * lamination_ratio) * (padded[1:] + padded[:-1])
    padded = jnp.pad(reluct, ((0, 0), (1, 1), (0, 0)))
    faces_x = 0.5 * (padded[:, 1:] + padded[:, :-1])
    padded = jnp.pad(reluct, ((0, 0), (0, 0), (1, 1)))
    faces_y = 0.5 * (padded[:, :, 1:] + padded[:, :, :-1])
    summed = faces_z[1:] + faces_z[:-1] + faces_x[:, 1:] + faces_x[:, :-1] + faces_y[:, :, 1:] + faces_y[:, :, :-1]
    return faces_z, faces_x, faces_y, summed


def couple(field, faces_z, faces_x, faces_y):
    padded = jnp.pad(field, ((0, 0), (1, 1), (0, 0), (0, 0)))
    result = faces_z[1:] * padded[:, 2:] + faces_z[:-1] * padded[:, :-2]
    padded = jnp.pad(field, ((0, 0), (0, 0), (1, 1), (0, 0)))
    result = result + faces_x[:, 1:] * padded[:, :, 2:] + faces_x[:, :-1] * padded[:, :, :-2]
    padded = jnp.pad(field, ((0, 0), (0, 0), (0, 0), (1, 1)))
    result = result + faces_y[:, :, 1:] * padded[:, :, :, 2:] + faces_y[:, :, :-1] * padded[:, :, :, :-2]
    return result


def reference(source, coarse_start, region, reluctivity, conductance):
    reluct = lookup(region, reluctivity)
    conduct = lookup(region, conductance)
    faces_z, faces_x, faces_y, summed = face_terms(reluct)
    fine_divisor = conduct + summed
    coarse_divisor = conduct / FINE + summed

    def sweeps(field, driving, divisor):
        for sweep_index in range(SWEEPS):
            field = (driving + couple(field, faces_z, faces_x, faces_y)) / divisor
        return field

    def fine_step(field, forcing):
        return sweeps(field, conduct * field + forcing, fine_divisor)

    def coarse_step(field):
        return sweeps(field, conduct / FINE * field, coarse_divisor)

    blocks = source.reshape((COARSE, FINE) + source.shape[1:])

    def relax_block(paired):
        start_state, forcings = paired

        def advance_one(field, forcing):
            result = fine_step(field, forcing)
            return result, result

        final_state, later_states = lax.scan(advance_one, start_state, forcings[1:])
        return jnp.concatenate([start_state[None], later_states], axis=0)

    states = lax.map(relax_block, (coarse_start, blocks))
    prev_last = jnp.roll(states[:, FINE - 1], 1, axis=0)
    arrived = lax.map(lambda paired: fine_step(paired[0], paired[1]), (prev_last, blocks[:, 0]))
    residual = arrived - states[:, 0]

    def coarse_turn(carried, defect):
        update = coarse_step(carried) + defect
        return update, update

    final_update, correction = lax.scan(coarse_turn, residual[COARSE - 1], residual)
    states = states.at[:, 0].add(correction)
    return states.reshape(source.shape)
```

```python
import functools

import jax
import jax.numpy as jnp
from jax import lax
from jax.experimental import pallas as pl
from jax.experimental.pallas import tpu as pltpu
from jax.sharding import PartitionSpec as P

SWEEPS = 4
COMP = 3
LAMINATION = 8.0
MESH = pl.DeviceIdType.MESH


def respond(first, drive, coef, own):
    planes = len(drive)
    current = {SWEEPS + p: first[p] for p in range(planes)} if first is not None else None
    for _ in range(SWEEPS):
        if current is None:
            current = {SWEEPS + p: drive[p] for p in range(planes)}
            continue
        after = {}

        def add(plane, term):
            after[plane] = after[plane] + term if plane in after else term

        for plane in range(planes):
            add(SWEEPS + plane, drive[plane])
        for q, value in current.items():
            add(q + 1, coef[0, q] * value)
            add(q - 1, coef[1, q] * value)
        for q, value in current.items():
            inplane = pltpu.roll(coef[2, q] * value, 1, 0) + pltpu.roll(coef[3, q] * value, 7, 0)
            inplane2 = pltpu.roll(coef[4, q] * value, 1, 1) + pltpu.roll(
                coef[5, q] * value, coef.shape[-1] - 1, 1
            )
            add(q, inplane + inplane2)
        current = after
    return current


def kernel(
    tms,
    spaces,
    src,
    start,
    region,
    reluctivity,
    conductance,
    out,
    sent,
    landed,
    own,
    base,
    mat_own,
    mat_far,
    fine_coef,
    coarse_coef,
    cell,
    turn_sent,
    turn_landed,
    mat_ssem,
    mat_rsem,
    ssem,
    rsem,
    turn_ssem,
    turn_rsem,
):
    fine, _, planes, rows, lanes = src.shape
    tm = lax.axis_index("tm")
    me = lax.axis_index("space")
    has_left = me > 0
    has_right = me < spaces - 1
    after_tm = lax.rem(tm + 1, tms)
    before_tm = lax.rem(tm + tms - 1, tms)

    def on_side(side):
        return has_left if side == 0 else has_right

    barrier = pltpu.get_barrier_semaphore()
    for row in (after_tm, before_tm):
        pl.semaphore_signal(barrier, inc=1, device_id=(row, me), device_id_type=MESH)
    for side, step in ((0, -1), (1, 1)):

        @pl.when(on_side(side))
        def _():
            for row in (tm, after_tm, before_tm):
                pl.semaphore_signal(barrier, inc=1, device_id=(row, me + step), device_id_type=MESH)

    for p in range(planes):
        kind = region[p]
        nu = jnp.zeros((rows, lanes), jnp.float32)
        s = jnp.zeros((rows, lanes), jnp.float32)
        for level in range(reluctivity.shape[0]):
            match = kind == level
            nu = jnp.where(match, reluctivity[level], nu)
            s = jnp.where(match, conductance[level], s)
        mat_own[0, p] = nu
        mat_own[1, p] = s

    zero = jnp.zeros((rows, lanes), jnp.float32)
    for side in (0, 1):

        @pl.when(jnp.logical_not(on_side(side)))
        def _():
            mat_far[side] = jnp.zeros(mat_far.shape[1:], jnp.float32)
            turn_landed[0, 2 * side] = jnp.zeros(turn_landed.shape[2:], jnp.float32)
            turn_landed[1, 2 * side] = jnp.zeros(turn_landed.shape[2:], jnp.float32)

            def clear(slot, carry):
                landed[slot, side] = jnp.zeros(landed.shape[2:], jnp.float32)
                return carry

            lax.fori_loop(0, fine, clear, 0)

    neighbours = 2 + 3 * has_left.astype(jnp.int32) + 3 * has_right.astype(jnp.int32)
    pl.semaphore_wait(barrier, neighbours)

    def far_side(side):
        return me - 1 if side == 0 else me + 1

    def mat_copy(side):
        return pltpu.make_async_remote_copy(
            src_ref=mat_own,
            dst_ref=mat_far.at[1 - side],
            send_sem=mat_ssem.at[side],
            recv_sem=mat_rsem.at[1 - side],
            device_id=(tm, far_side(side)),
            device_id_type=MESH,
        )

    def mat_arrival(side):
        return pltpu.make_async_remote_copy(
            src_ref=mat_own,
            dst_ref=mat_far.at[side],
            send_sem=mat_ssem.at[side],
            recv_sem=mat_rsem.at[side],
            device_id=(tm, far_side(side)),
            device_id_type=MESH,
        )

    def part_copy(slot, side, c, arrival=False):
        other = side if arrival else 1 - side
        return pltpu.make_async_remote_copy(
            src_ref=sent.at[slot, side, c],
            dst_ref=landed.at[slot, other, c],
            send_sem=ssem.at[slot, side, c],
            recv_sem=rsem.at[slot, other, c],
            device_id=(tm, far_side(side)),
            device_id_type=MESH,
        )

    def turn_copy(phase, piece, c, arrival=False):
        other = piece if arrival else 2 - piece
        return pltpu.make_async_remote_copy(
            src_ref=turn_sent.at[phase, piece, c],
            dst_ref=turn_landed.at[phase, other, c],
            send_sem=turn_ssem.at[phase, piece, c],
            recv_sem=turn_rsem.at[phase, other, c],
            device_id=(after_tm, me + piece - 1),
            device_id_type=MESH,
        )

    def with_piece(piece, act):
        if piece == 1:
            act()
        else:
            pl.when(on_side(piece // 2))(act)

    for side in (0, 1):
        pl.when(on_side(side))(lambda side=side: mat_copy(side).start())
    for side in (0, 1):
        pl.when(on_side(side))(lambda side=side: mat_arrival(side).wait_recv())

    nus = [mat_far[0, 0, p] for p in range(planes)]
    nus += [mat_own[0, p] for p in range(planes)]
    nus += [mat_far[1, 0, p] for p in range(planes)]
    ss = [mat_far[0, 1, p] for p in range(planes)]
    ss += [mat_own[1, p] for p in range(planes)]
    ss += [mat_far[1, 1, p] for p in range(planes)]
    row_at = lax.broadcasted_iota(jnp.int32, (rows, lanes), 0)
    lane_at = lax.broadcasted_iota(jnp.int32, (rows, lanes), 1)
    one = jnp.float32(1.0)
    inside = [has_left.astype(jnp.float32)] * planes + [one] * planes
    inside += [has_right.astype(jnp.float32)] * planes
    for q in range(1, 3 * planes - 1):
        nu, s = nus[q], ss[q]
        up_z = (0.5 * LAMINATION) * (nus[q + 1] + nu)
        down_z = (0.5 * LAMINATION) * (nus[q - 1] + nu)
        up_x = 0.5 * (nu + jnp.where(row_at < rows - 1, pltpu.roll(nu, rows - 1, 0), 0.0))
        down_x = 0.5 * (nu + jnp.where(row_at > 0, pltpu.roll(nu, 1, 0), 0.0))
        up_y = 0.5 * (nu + jnp.where(lane_at < lanes - 1, pltpu.roll(nu, lanes - 1, 1), 0.0))
        down_y = 0.5 * (nu + jnp.where(lane_at > 0, pltpu.roll(nu, 1, 1), 0.0))
        summed = up_z + down_z + up_x + down_x + up_y + down_y
        gives = [
            up_z,
            down_z,
            jnp.where(row_at < rows - 1, up_x, 0.0),
            jnp.where(row_at > 0, down_x, 0.0),
            jnp.where(lane_at < lanes - 1, up_y, 0.0),
            jnp.where(lane_at > 0, down_y, 0.0),
        ]
        outside = 1.0 - inside[q]
        fine_d = s + summed
        coarse_d = s / fine + summed
        fine_inv = inside[q] / (fine_d + outside)
        coarse_inv = inside[q] / (coarse_d + outside)
        for which in range(6):
            fine_coef[which, q] = gives[which] * fine_inv
            coarse_coef[which, q] = gives[which] * coarse_inv
        if planes <= q < 2 * planes:
            p = q - planes
            cell[0, p] = fine_inv
            cell[1, p] = s * fine_inv
            cell[2, p] = fine_d
            cell[3, p] = coarse_inv
            cell[4, p] = s / fine * coarse_inv
            cell[5, p] = coarse_d

    def spread(reach, slot, c):
        for p in range(planes):
            sent[slot, 0, c, p] = reach[p] if p in reach else zero
            sent[slot, 1, c, p] = reach[2 * planes + p] if 2 * planes + p in reach else zero
        for side in (0, 1):
            pl.when(on_side(side))(lambda side=side: part_copy(slot, side, c).start())

    def gathered(slot, c):
        for side in (0, 1):
            pl.when(on_side(side))(lambda side=side: part_copy(slot, side, c, True).wait_recv())
        return [landed[slot, 0, c, p] + landed[slot, 1, c, p] for p in range(planes)]

    def turn_spread(reach, phase, c):
        for piece in range(3):
            for p in range(planes):
                turn_sent[phase, piece, c, p] = reach[piece * planes + p]
        for piece in range(3):
            with_piece(piece, lambda piece=piece: turn_copy(phase, piece, c).start())

    def turn_gathered(phase, c):
        for piece in range(3):
            with_piece(piece, lambda piece=piece: turn_copy(phase, piece, c, True).wait_recv())
        return [
            turn_landed[phase, 0, c, p] + turn_landed[phase, 1, c, p] + turn_landed[phase, 2, c, p]
            for p in range(planes)
        ]

    for c in range(COMP):
        first = [cell[2, p] * start[0, c, p] for p in range(planes)]
        drive = [cell[1, p] * first[p] + src[1, c, p] for p in range(planes)]
        reach = respond(first, drive, fine_coef, own)
        spread(reach, 1, c)
        for p in range(planes):
            own[c, p] = reach[planes + p]

    for c in range(COMP):
        reach = respond(None, [src[0, c, p] for p in range(planes)], fine_coef, own)
        spread(reach, 0, c)
        for p in range(planes):
            base[c, p] = reach[planes + p] - cell[2, p] * start[0, c, p]

    def one_step(j, carry):
        for c in range(COMP):
            arrived = gathered(j - 1, c)
            first = [own[c, p] + arrived[p] for p in range(planes)]
            drive = [cell[1, p] * first[p] + src[j, c, p] for p in range(planes)]
            reach = respond(first, drive, fine_coef, own)
            spread(reach, j, c)
            for p in range(planes):
                own[c, p] = reach[planes + p]
                out[j - 1, c, p] = first[p] * cell[0, p]
        return carry

    lax.fori_loop(2, fine, one_step, 0)

    for c in range(COMP):
        arrived = gathered(fine - 1, c)
        first = [own[c, p] + arrived[p] for p in range(planes)]
        drive = [cell[1, p] * first[p] for p in range(planes)]
        turn_spread(respond(first, drive, fine_coef, own), 0, c)
        for p in range(planes):
            out[fine - 1, c, p] = first[p] * cell[0, p]

    for c in range(COMP):
        arrived = gathered(0, c)
        for p in range(planes):
            base[c, p] = base[c, p] + arrived[p]

    last = tm == tms - 1
    for c in range(COMP):
        arrived = turn_gathered(0, c)
        for p in range(planes):
            base[c, p] = (base[c, p] + arrived[p]) * cell[0, p] * cell[5, p]

        @pl.when(last)
        def _():
            first = [base[c, p] for p in range(planes)]
            drive = [cell[4, p] * first[p] for p in range(planes)]
            turn_spread(respond(first, drive, coarse_coef, own), 1, c)

    for c in range(COMP):
        arrived = turn_gathered(1, c)
        for p in range(planes):
            base[c, p] = base[c, p] + arrived[p]

        @pl.when(jnp.logical_not(last))
        def _():
            first = [base[c, p] for p in range(planes)]
            drive = [cell[4, p] * first[p] for p in range(planes)]
            turn_spread(respond(first, drive, coarse_coef, own), 1, c)

        for p in range(planes):
            out[0, c, p] = start[0, c, p] + base[c, p] * cell[3, p]

    for side in (0, 1):

        @pl.when(on_side(side))
        def _():
            mat_copy(side).wait_send()

            def left(slot, carry):
                for c in range(COMP):
                    part_copy(slot, side, c).wait_send()
                return carry

            lax.fori_loop(0, fine, left, 0)

    for phase in (0, 1):
        for piece in range(3):
            for c in range(COMP):
                with_piece(piece, lambda: turn_copy(phase, piece, c).wait_send())


def local(source, coarse_start, region, reluctivity, conductance):
    fine, comp, planes, rows, lanes = source.shape
    vmem = pl.BlockSpec(memory_space=pltpu.VMEM)
    smem = pl.BlockSpec(memory_space=pltpu.SMEM)
    slab = (planes, rows, lanes)
    return pl.pallas_call(
        functools.partial(kernel, lax.axis_size("tm"), lax.axis_size("space")),
        out_shape=jax.ShapeDtypeStruct(source.shape, source.dtype),
        in_specs=[vmem, vmem, vmem, smem, smem],
        out_specs=vmem,
        scratch_shapes=[
            pltpu.VMEM((fine, 2, comp) + slab, jnp.float32),
            pltpu.VMEM((fine, 2, comp) + slab, jnp.float32),
            pltpu.VMEM((comp,) + slab, jnp.float32),
            pltpu.VMEM((comp,) + slab, jnp.float32),
            pltpu.VMEM((2,) + slab, jnp.float32),
            pltpu.VMEM((2, 2) + slab, jnp.float32),
            pltpu.VMEM((6, 3 * planes, rows, lanes), jnp.float32),
            pltpu.VMEM((6, 3 * planes, rows, lanes), jnp.float32),
            pltpu.VMEM((6,) + slab, jnp.float32),
            pltpu.VMEM((2, 3, comp) + slab, jnp.float32),
            pltpu.VMEM((2, 3, comp) + slab, jnp.float32),
            pltpu.SemaphoreType.DMA((2,)),
            pltpu.SemaphoreType.DMA((2,)),
            pltpu.SemaphoreType.DMA((fine, 2, comp)),
            pltpu.SemaphoreType.DMA((fine, 2, comp)),
            pltpu.SemaphoreType.DMA((2, 3, comp)),
            pltpu.SemaphoreType.DMA((2, 3, comp)),
        ],
        compiler_params=pltpu.CompilerParams(
            collective_id=0, has_side_effects=True, vmem_limit_bytes=32 * 1024 * 1024
        ),
        cost_estimate=pl.CostEstimate(
            flops=20_000_000, bytes_accessed=1_800_000, transcendentals=0
        ),
    )(source, coarse_start, region, reluctivity, conductance)


def solution(mesh):
    placed = (
        P("tm", None, "space", None, None),
        P("tm", None, "space", None, None),
        P("space", None, None),
        P(),
        P(),
    )
    return jax.shard_map(
        local,
        mesh=mesh,
        in_specs=placed,
        out_specs=P("tm", None, "space", None, None),
        check_vma=False,
    )
```

```python
import functools

import jax
import jax.numpy as jnp
from jax import lax
from jax.experimental import pallas as pl
from jax.experimental.pallas import tpu as pltpu
from jax.sharding import PartitionSpec as P

SWEEPS = 4
COMP = 3
LAMINATION = 8.0
SHIFTS = (-2, -1, 1, 2)
MESH = pl.DeviceIdType.MESH


def respond(first, drive, coef):
    current = first
    for _ in range(SWEEPS):
        if current is None:
            current = dict(drive)
            continue
        after = dict(drive)

        def add(plane, term):
            after[plane] = after[plane] + term if plane in after else term

        for q, value in current.items():
            add(q + 1, coef[0, q] * value)
            add(q - 1, coef[1, q] * value)
        for q, value in current.items():
            in_x = pltpu.roll(coef[2, q] * value, 1, 0) + pltpu.roll(coef[3, q] * value, 7, 0)
            in_y = pltpu.roll(coef[4, q] * value, 1, 1) + pltpu.roll(
                coef[5, q] * value, coef.shape[-1] - 1, 1
            )
            add(q, in_x + in_y)
        current = after
    return current


def kernel(
    tms,
    spaces,
    src,
    start,
    region,
    reluctivity,
    conductance,
    out,
    sent,
    landed,
    own,
    base,
    mat_own,
    mat_far,
    fine_coef,
    coarse_coef,
    pull,
    cell,
    turn_sent,
    turn_landed,
    mat_ssem,
    mat_rsem,
    ssem,
    rsem,
    turn_ssem,
    turn_rsem,
):
    fine, _, planes, rows, lanes = src.shape
    tm = lax.axis_index("tm")
    me = lax.axis_index("space")
    after_tm = lax.rem(tm + 1, tms)
    before_tm = lax.rem(tm + tms - 1, tms)
    mid = 2 * planes

    def reaches(shift):
        return me + shift >= 0 if shift < 0 else me + shift < spaces

    barrier = pltpu.get_barrier_semaphore()
    for row in (after_tm, before_tm):
        pl.semaphore_signal(barrier, inc=1, device_id=(row, me), device_id_type=MESH)
    neighbours = jnp.int32(2)
    for shift in SHIFTS:
        neighbours = neighbours + 3 * reaches(shift).astype(jnp.int32)

        @pl.when(reaches(shift))
        def _():
            for row in (tm, after_tm, before_tm):
                pl.semaphore_signal(barrier, inc=1, device_id=(row, me + shift), device_id_type=MESH)

    for p in range(planes):
        kind = region[p]
        nu = jnp.zeros((rows, lanes), jnp.float32)
        s = jnp.zeros((rows, lanes), jnp.float32)
        for level in range(reluctivity.shape[0]):
            match = kind == level
            nu = jnp.where(match, reluctivity[level], nu)
            s = jnp.where(match, conductance[level], s)
        mat_own[0, p] = nu
        mat_own[1, p] = s

    zero = jnp.zeros((rows, lanes), jnp.float32)
    for at, shift in enumerate(SHIFTS):

        @pl.when(jnp.logical_not(reaches(shift)))
        def _():
            mat_far[at] = jnp.zeros(mat_far.shape[1:], jnp.float32)
            for phase in (0, 1):
                turn_landed[phase, 2 + shift] = jnp.zeros(turn_landed.shape[2:], jnp.float32)

            def clear(slot, carry):
                landed[slot, at] = jnp.zeros(landed.shape[2:], jnp.float32)
                return carry

            lax.fori_loop(0, fine, clear, 0)

    pl.semaphore_wait(barrier, neighbours)

    def mat_copy(at, arrival=False):
        other = at if arrival else 3 - at
        return pltpu.make_async_remote_copy(
            src_ref=mat_own,
            dst_ref=mat_far.at[other],
            send_sem=mat_ssem.at[at],
            recv_sem=mat_rsem.at[other],
            device_id=(tm, me + SHIFTS[at]),
            device_id_type=MESH,
        )

    def part_copy(slot, at, c, arrival=False):
        other = at if arrival else 3 - at
        return pltpu.make_async_remote_copy(
            src_ref=sent.at[slot, at, c],
            dst_ref=landed.at[slot, other, c],
            send_sem=ssem.at[slot, at, c],
            recv_sem=rsem.at[slot, other, c],
            device_id=(tm, me + SHIFTS[at]),
            device_id_type=MESH,
        )

    def turn_copy(phase, piece, c, arrival=False):
        other = piece if arrival else 4 - piece
        return pltpu.make_async_remote_copy(
            src_ref=turn_sent.at[phase, piece, c],
            dst_ref=turn_landed.at[phase, other, c],
            send_sem=turn_ssem.at[phase, piece, c],
            recv_sem=turn_rsem.at[phase, other, c],
            device_id=(after_tm, me + piece - 2),
            device_id_type=MESH,
        )

    def with_piece(piece, act):
        if piece == 2:
            act()
        else:
            pl.when(reaches(piece - 2))(act)

    for at in (1, 2, 0, 3):
        pl.when(reaches(SHIFTS[at]))(lambda at=at: mat_copy(at).start())
    for at in (1, 2, 0, 3):
        pl.when(reaches(SHIFTS[at]))(lambda at=at: mat_copy(at, True).wait_recv())

    def whole(kind):
        gathered_planes = []
        for at in (0, 1, None, 2, 3):
            for p in range(planes):
                gathered_planes.append(mat_own[kind, p] if at is None else mat_far[at, kind, p])
        return gathered_planes

    nus, ss = whole(0), whole(1)
    row_at = lax.broadcasted_iota(jnp.int32, (rows, lanes), 0)
    lane_at = lax.broadcasted_iota(jnp.int32, (rows, lanes), 1)
    inside = []
    for shift in (-2, -1, 0, 1, 2):
        held = reaches(shift).astype(jnp.float32) if shift else jnp.float32(1.0)
        inside += [held] * planes
    for q in range(1, 5 * planes - 1):
        nu, s = nus[q], ss[q]
        up_z = (0.5 * LAMINATION) * (nus[q + 1] + nu)
        down_z = (0.5 * LAMINATION) * (nus[q - 1] + nu)
        up_x = 0.5 * (nu + jnp.where(row_at < rows - 1, pltpu.roll(nu, rows - 1, 0), 0.0))
        down_x = 0.5 * (nu + jnp.where(row_at > 0, pltpu.roll(nu, 1, 0), 0.0))
        up_y = 0.5 * (nu + jnp.where(lane_at < lanes - 1, pltpu.roll(nu, lanes - 1, 1), 0.0))
        down_y = 0.5 * (nu + jnp.where(lane_at > 0, pltpu.roll(nu, 1, 1), 0.0))
        summed = up_z + down_z + up_x + down_x + up_y + down_y
        gives = [
            up_z,
            down_z,
            jnp.where(row_at < rows - 1, up_x, 0.0),
            jnp.where(row_at > 0, down_x, 0.0),
            jnp.where(lane_at < lanes - 1, up_y, 0.0),
            jnp.where(lane_at > 0, down_y, 0.0),
        ]
        outside = 1.0 - inside[q]
        fine_d = s + summed
        coarse_d = s / fine + summed
        fine_inv = inside[q] / (fine_d + outside)
        coarse_inv = inside[q] / (coarse_d + outside)
        pull[q] = s * fine_inv
        for which in range(6):
            fine_coef[which, q] = gives[which] * fine_inv
            if planes < q < 4 * planes - 1:
                coarse_coef[which, q] = gives[which] * coarse_inv
        if mid <= q < mid + planes:
            p = q - mid
            cell[0, p] = fine_inv
            cell[2, p] = fine_d
            cell[3, p] = coarse_inv
            cell[4, p] = s / fine * coarse_inv
            cell[5, p] = coarse_d

    def store(reach, slot, at, c):
        begin = mid + SHIFTS[at] * planes
        for p in range(planes):
            sent[slot, at, c, p] = reach[begin + p] if begin + p in reach else zero

    def ship(slot, at, c):
        pl.when(reaches(SHIFTS[at]))(lambda: part_copy(slot, at, c).start())

    def gathered(slot, c, sides):
        for at in sides:
            pl.when(reaches(SHIFTS[at]))(lambda at=at: part_copy(slot, at, c, True).wait_recv())
        total = []
        for p in range(planes):
            value = landed[slot, sides[0], c, p]
            for at in sides[1:]:
                value = value + landed[slot, at, c, p]
            total.append(value)
        return total

    def turn_spread(reach, phase, c, pieces):
        for piece in pieces:
            for p in range(planes):
                turn_sent[phase, piece, c, p] = reach[piece * planes + p]
        for piece in pieces:
            with_piece(piece, lambda piece=piece: turn_copy(phase, piece, c).start())

    def turn_gathered(phase, c, pieces):
        for piece in pieces:
            with_piece(piece, lambda piece=piece: turn_copy(phase, piece, c, True).wait_recv())
        total = []
        for p in range(planes):
            value = turn_landed[phase, pieces[0], c, p]
            for piece in pieces[1:]:
                value = value + turn_landed[phase, piece, c, p]
            total.append(value)
        return total

    near, every = (1, 2), (0, 1, 2, 3)
    span = range(planes)

    def fine_drive(state, slot, c):
        drive = {q: pull[q] * value for q, value in state.items()}
        if slot is not None:
            for p in span:
                drive[mid + p] = drive[mid + p] + src[slot, c, p]
        return drive

    def two_steps(values, slot, c, final=False):
        state = {mid + p: values[p] for p in span}
        halfway = respond(state, fine_drive(state, slot, c), fine_coef)
        reach = respond(
            halfway, fine_drive(halfway, None if final else slot + 1, c), fine_coef
        )
        for at in near:
            store(halfway, slot, at, c)
        if final:
            turn_spread(reach, 0, c, range(5))
        else:
            for at in every:
                store(reach, slot + 1, at, c)
            for at in every:
                ship(slot + 1, at, c)
            for p in span:
                own[c, p] = reach[mid + p]
        for at in near:
            ship(slot, at, c)
        for p in span:
            out[slot, c, p] = halfway[mid + p]

    for c in range(COMP):
        two_steps([cell[2, p] * start[0, c, p] for p in span], 1, c)

    for c in range(COMP):
        reach = respond(None, {mid + p: src[0, c, p] for p in span}, fine_coef)
        for at in near:
            store(reach, 0, at, c)
        for at in near:
            ship(0, at, c)
        for p in span:
            base[c, p] = reach[mid + p] - cell[2, p] * start[0, c, p]

    def arrive(slot, c):
        arrived = gathered(slot, c, every)
        values = [own[c, p] + arrived[p] for p in span]
        for p in span:
            out[slot, c, p] = values[p] * cell[0, p]
        return values

    def one_pair(pair, carry):
        for c in range(COMP):
            two_steps(arrive(2 * pair, c), 2 * pair + 1, c)
        return carry

    lax.fori_loop(1, fine // 2 - 1, one_pair, 0)
    for c in range(COMP):
        two_steps(arrive(fine - 2, c), fine - 1, c, True)

    def finish(slot):
        for c in range(COMP):
            arrived = gathered(slot, c, near)
            for p in span:
                out[slot, c, p] = (out[slot, c, p] + arrived[p]) * cell[0, p]

    for c in range(COMP):
        arrived = gathered(0, c, near)
        for p in span:
            base[c, p] = base[c, p] + arrived[p]

    def finish_pair(pair, carry):
        finish(2 * pair + 1)
        return carry

    lax.fori_loop(0, fine // 2 - 1, finish_pair, 0)

    last = tm == tms - 1
    inner = (1, 2, 3)

    def coarse_turn(c):
        first = {mid + p: base[c, p] for p in span}
        drive = {mid + p: cell[4, p] * base[c, p] for p in span}
        turn_spread(respond(first, drive, coarse_coef), 1, c, inner)

    for c in range(COMP):
        arrived = turn_gathered(0, c, range(5))
        for p in span:
            base[c, p] = (base[c, p] + arrived[p]) * cell[0, p] * cell[5, p]
        pl.when(last)(lambda c=c: coarse_turn(c))

    for c in range(COMP):
        arrived = turn_gathered(1, c, inner)
        for p in span:
            base[c, p] = base[c, p] + arrived[p]
        pl.when(jnp.logical_not(last))(lambda c=c: coarse_turn(c))
        for p in span:
            out[0, c, p] = start[0, c, p] + base[c, p] * cell[3, p]
    finish(fine - 1)

    for at in every:

        @pl.when(reaches(SHIFTS[at]))
        def _():
            mat_copy(at).wait_send()

            def left(slot, carry):
                for c in range(COMP):
                    part_copy(slot if at in near else 2 * slot, at, c).wait_send()
                return carry

            if at in near:
                lax.fori_loop(0, fine, left, 0)
            else:
                lax.fori_loop(1, fine // 2, left, 0)

    for phase in (0, 1):
        for piece in range(5) if phase == 0 else inner:
            for c in range(COMP):
                with_piece(piece, lambda: turn_copy(phase, piece, c).wait_send())


def local(source, coarse_start, region, reluctivity, conductance):
    fine, comp, planes, rows, lanes = source.shape
    vmem = pl.BlockSpec(memory_space=pltpu.VMEM)
    smem = pl.BlockSpec(memory_space=pltpu.SMEM)
    slab = (planes, rows, lanes)
    return pl.pallas_call(
        functools.partial(kernel, lax.axis_size("tm"), lax.axis_size("space")),
        out_shape=jax.ShapeDtypeStruct(source.shape, source.dtype),
        in_specs=[vmem, vmem, vmem, smem, smem],
        out_specs=vmem,
        scratch_shapes=[
            pltpu.VMEM((fine, 4, comp) + slab, jnp.float32),
            pltpu.VMEM((fine, 4, comp) + slab, jnp.float32),
            pltpu.VMEM((comp,) + slab, jnp.float32),
            pltpu.VMEM((comp,) + slab, jnp.float32),
            pltpu.VMEM((2,) + slab, jnp.float32),
            pltpu.VMEM((4, 2) + slab, jnp.float32),
            pltpu.VMEM((6, 5 * planes, rows, lanes), jnp.float32),
            pltpu.VMEM((6, 5 * planes, rows, lanes), jnp.float32),
            pltpu.VMEM((5 * planes, rows, lanes), jnp.float32),
            pltpu.VMEM((6,) + slab, jnp.float32),
            pltpu.VMEM((2, 5, comp) + slab, jnp.float32),
            pltpu.VMEM((2, 5, comp) + slab, jnp.float32),
            pltpu.SemaphoreType.DMA((4,)),
            pltpu.SemaphoreType.DMA((4,)),
            pltpu.SemaphoreType.DMA((fine, 4, comp)),
            pltpu.SemaphoreType.DMA((fine, 4, comp)),
            pltpu.SemaphoreType.DMA((2, 5, comp)),
            pltpu.SemaphoreType.DMA((2, 5, comp)),
        ],
        compiler_params=pltpu.CompilerParams(
            collective_id=0, has_side_effects=True, vmem_limit_bytes=32 * 1024 * 1024
        ),
        cost_estimate=pl.CostEstimate(
            flops=20_000_000, bytes_accessed=1_800_000, transcendentals=0
        ),
    )(source, coarse_start, region, reluctivity, conductance)


def solution(mesh):
    placed = (
        P("tm", None, "space", None, None),
        P("tm", None, "space", None, None),
        P("space", None, None),
        P(),
        P(),
    )
    return jax.shard_map(
        local,
        mesh=mesh,
        in_specs=placed,
        out_specs=P("tm", None, "space", None, None),
        check_vma=False,
    )
```

```python
import functools

import jax
import jax.numpy as jnp
from jax import lax
from jax.experimental import pallas as pl
from jax.experimental.pallas import tpu as pltpu
from jax.sharding import PartitionSpec as P

SWEEPS = 4
COMP = 3
LAMINATION = 8.0
SHIFTS = (-2, -1, 1, 2)
MESH = pl.DeviceIdType.MESH


def respond(first, drive, coef):
    current = first
    for _ in range(SWEEPS):
        if current is None:
            current = dict(drive)
            continue
        after = dict(drive)

        def add(plane, term):
            after[plane] = after[plane] + term if plane in after else term

        for q, value in current.items():
            add(q + 1, coef[0, q] * value)
            add(q - 1, coef[1, q] * value)
        for q, value in current.items():
            in_x = pltpu.roll(coef[2, q] * value, 1, 0) + pltpu.roll(coef[3, q] * value, 7, 0)
            in_y = pltpu.roll(coef[4, q] * value, 1, 1) + pltpu.roll(
                coef[5, q] * value, coef.shape[-1] - 1, 1
            )
            add(q, in_x + in_y)
        current = after
    return current


def kernel(
    tms,
    spaces,
    src_in,
    start_in,
    region_in,
    reluctivity_in,
    conductance_in,
    out,
    src,
    start,
    region,
    reluctivity,
    conductance,
    in_sem,
    sent,
    landed,
    own,
    base,
    mat_own,
    mat_far,
    fine_coef,
    coarse_coef,
    pull,
    coarse_pull,
    cell,
    turn_sent,
    turn_landed,
    mat_ssem,
    mat_rsem,
    ssem,
    rsem,
    turn_ssem,
    turn_rsem,
):
    fine, _, planes, rows, lanes = src.shape
    loads = [
        pltpu.make_async_copy(held, kept, in_sem.at[i])
        for i, (held, kept) in enumerate(
            (
                (reluctivity_in, reluctivity),
                (conductance_in, conductance),
                (region_in, region),
                (start_in, start),
                (src_in, src),
            )
        )
    ]
    for load in loads:
        load.start()
    tm = lax.axis_index("tm")
    me = lax.axis_index("space")
    after_tm = lax.rem(tm + 1, tms)
    before_tm = lax.rem(tm + tms - 1, tms)
    after_two = lax.rem(tm + 2, tms)
    before_two = lax.rem(tm + tms - 2, tms)
    mid = 2 * planes

    def reaches(shift):
        return me + shift >= 0 if shift < 0 else me + shift < spaces

    barrier = pltpu.get_barrier_semaphore()
    others = (after_tm, before_tm, after_two, before_two)
    for row in others:
        pl.semaphore_signal(barrier, inc=1, device_id=(row, me), device_id_type=MESH)
    neighbours = jnp.int32(4)
    for shift in SHIFTS:
        neighbours = neighbours + 5 * reaches(shift).astype(jnp.int32)

        @pl.when(reaches(shift))
        def _():
            for row in (tm,) + others:
                pl.semaphore_signal(barrier, inc=1, device_id=(row, me + shift), device_id_type=MESH)

    for load in loads[:3]:
        load.wait()
    for p in range(planes):
        kind = region[p]
        nu = jnp.zeros((rows, lanes), jnp.float32)
        s = jnp.zeros((rows, lanes), jnp.float32)
        for level in range(reluctivity.shape[0]):
            match = kind == level
            nu = jnp.where(match, reluctivity[level], nu)
            s = jnp.where(match, conductance[level], s)
        mat_own[0, p] = nu
        mat_own[1, p] = s

    zero = jnp.zeros((rows, lanes), jnp.float32)
    for at, shift in enumerate(SHIFTS):

        @pl.when(jnp.logical_not(reaches(shift)))
        def _():
            mat_far[at] = jnp.zeros(mat_far.shape[1:], jnp.float32)
            for phase in (0, 1, 2):
                turn_landed[phase, 2 + shift] = jnp.zeros(turn_landed.shape[2:], jnp.float32)

            def clear(slot, carry):
                landed[slot, at] = jnp.zeros(landed.shape[2:], jnp.float32)
                return carry

            lax.fori_loop(0, fine, clear, 0)

    pl.semaphore_wait(barrier, neighbours)

    def mat_copy(at, arrival=False):
        other = at if arrival else 3 - at
        return pltpu.make_async_remote_copy(
            src_ref=mat_own,
            dst_ref=mat_far.at[other],
            send_sem=mat_ssem.at[at],
            recv_sem=mat_rsem.at[other],
            device_id=(tm, me + SHIFTS[at]),
            device_id_type=MESH,
        )

    def whole_copy(slot, at, arrival=False):
        other = at if arrival else 3 - at
        return pltpu.make_async_remote_copy(
            src_ref=sent.at[slot, at],
            dst_ref=landed.at[slot, other],
            send_sem=ssem.at[slot, at, 0],
            recv_sem=rsem.at[slot, other, 0],
            device_id=(tm, me + SHIFTS[at]),
            device_id_type=MESH,
        )

    def part_copy(slot, at, c, arrival=False):
        other = at if arrival else 3 - at
        return pltpu.make_async_remote_copy(
            src_ref=sent.at[slot, at, c],
            dst_ref=landed.at[slot, other, c],
            send_sem=ssem.at[slot, at, c],
            recv_sem=rsem.at[slot, other, c],
            device_id=(tm, me + SHIFTS[at]),
            device_id_type=MESH,
        )

    def turn_copy(phase, piece, c, arrival=False):
        other = piece if arrival else 4 - piece
        return pltpu.make_async_remote_copy(
            src_ref=turn_sent.at[phase, piece, c],
            dst_ref=turn_landed.at[phase, other, c],
            send_sem=turn_ssem.at[phase, piece, c],
            recv_sem=turn_rsem.at[phase, other, c],
            device_id=(after_two if phase == 2 else after_tm, me + piece - 2),
            device_id_type=MESH,
        )

    def with_piece(piece, act):
        if piece == 2:
            act()
        else:
            pl.when(reaches(piece - 2))(act)

    for at in (1, 2, 0, 3):
        pl.when(reaches(SHIFTS[at]))(lambda at=at: mat_copy(at).start())
    for load in loads[3:]:
        load.wait()
    for at in (1, 2, 0, 3):
        pl.when(reaches(SHIFTS[at]))(lambda at=at: mat_copy(at, True).wait_recv())

    def whole(kind):
        gathered_planes = []
        for at in (0, 1, None, 2, 3):
            for p in range(planes):
                gathered_planes.append(mat_own[kind, p] if at is None else mat_far[at, kind, p])
        return gathered_planes

    nus, ss = whole(0), whole(1)
    row_at = lax.broadcasted_iota(jnp.int32, (rows, lanes), 0)
    lane_at = lax.broadcasted_iota(jnp.int32, (rows, lanes), 1)
    inside = []
    for shift in (-2, -1, 0, 1, 2):
        held = reaches(shift).astype(jnp.float32) if shift else jnp.float32(1.0)
        inside += [held] * planes
    for q in range(1, 5 * planes - 1):
        nu, s = nus[q], ss[q]
        up_z = (0.5 * LAMINATION) * (nus[q + 1] + nu)
        down_z = (0.5 * LAMINATION) * (nus[q - 1] + nu)
        up_x = 0.5 * (nu + jnp.where(row_at < rows - 1, pltpu.roll(nu, rows - 1, 0), 0.0))
        down_x = 0.5 * (nu + jnp.where(row_at > 0, pltpu.roll(nu, 1, 0), 0.0))
        up_y = 0.5 * (nu + jnp.where(lane_at < lanes - 1, pltpu.roll(nu, lanes - 1, 1), 0.0))
        down_y = 0.5 * (nu + jnp.where(lane_at > 0, pltpu.roll(nu, 1, 1), 0.0))
        summed = up_z + down_z + up_x + down_x + up_y + down_y
        gives = [
            up_z,
            down_z,
            jnp.where(row_at < rows - 1, up_x, 0.0),
            jnp.where(row_at > 0, down_x, 0.0),
            jnp.where(lane_at < lanes - 1, up_y, 0.0),
            jnp.where(lane_at > 0, down_y, 0.0),
        ]
        outside = 1.0 - inside[q]
        fine_d = s + summed
        coarse_d = s / fine + summed
        fine_inv = inside[q] / (fine_d + outside)
        coarse_inv = inside[q] / (coarse_d + outside)
        pull[q] = s * fine_inv
        coarse_pull[q] = s / fine * coarse_inv
        for which in range(6):
            fine_coef[which, q] = gives[which] * fine_inv
            coarse_coef[which, q] = gives[which] * coarse_inv
        if mid <= q < mid + planes:
            p = q - mid
            cell[0, p] = fine_inv
            cell[2, p] = fine_d
            cell[3, p] = coarse_inv
            cell[5, p] = coarse_d

    def store(reach, slot, at, c):
        begin = mid + SHIFTS[at] * planes
        for p in range(planes):
            sent[slot, at, c, p] = reach[begin + p] if begin + p in reach else zero

    def ship(slot, at, c):
        pl.when(reaches(SHIFTS[at]))(lambda: part_copy(slot, at, c).start())

    def ship_whole(slot):
        for at in near:
            pl.when(reaches(SHIFTS[at]))(lambda at=at: whole_copy(slot, at).start())

    def await_whole(slot):
        for at in near:
            pl.when(reaches(SHIFTS[at]))(lambda at=at: whole_copy(slot, at, True).wait_recv())

    def gathered(slot, c, sides):
        for at in sides:
            pl.when(reaches(SHIFTS[at]))(lambda at=at: part_copy(slot, at, c, True).wait_recv())
        return landed_sum(slot, c, sides)

    def landed_sum(slot, c, sides):
        total = []
        for p in range(planes):
            value = landed[slot, sides[0], c, p]
            for at in sides[1:]:
                value = value + landed[slot, at, c, p]
            total.append(value)
        return total

    def turn_spread(reach, phase, c, pieces):
        for piece in pieces:
            for p in range(planes):
                turn_sent[phase, piece, c, p] = reach[piece * planes + p]
        for piece in pieces:
            with_piece(piece, lambda piece=piece: turn_copy(phase, piece, c).start())

    def turn_gathered(phase, c, pieces):
        for piece in pieces:
            with_piece(piece, lambda piece=piece: turn_copy(phase, piece, c, True).wait_recv())
        total = []
        for p in range(planes):
            value = turn_landed[phase, pieces[0], c, p]
            for piece in pieces[1:]:
                value = value + turn_landed[phase, piece, c, p]
            total.append(value)
        return total

    near, every = (1, 2), (0, 1, 2, 3)
    span = range(planes)

    def fine_drive(state, slot, c):
        drive = {q: pull[q] * value for q, value in state.items()}
        if slot is not None:
            for p in span:
                drive[mid + p] = drive[mid + p] + src[slot, c, p]
        return drive

    def two_steps(values, slot, c, final=False):
        state = {mid + p: values[p] for p in span}
        halfway = respond(state, fine_drive(state, slot, c), fine_coef)
        reach = respond(
            halfway, fine_drive(halfway, None if final else slot + 1, c), fine_coef
        )
        for at in near:
            store(halfway, slot, at, c)
        if final:
            turn_spread(reach, 0, c, range(5))
        else:
            for at in every:
                store(reach, slot + 1, at, c)
            for at in every:
                ship(slot + 1, at, c)
            for p in span:
                own[c, p] = reach[mid + p]
        for p in span:
            out[slot, c, p] = halfway[mid + p]

    for c in range(COMP):
        two_steps([cell[2, p] * start[0, c, p] for p in span], 1, c)
    ship_whole(1)

    for c in range(COMP):
        reach = respond(None, {mid + p: src[0, c, p] for p in span}, fine_coef)
        for at in near:
            store(reach, 0, at, c)
        for p in span:
            base[c, p] = reach[mid + p] - cell[2, p] * start[0, c, p]
    ship_whole(0)

    def arrive(slot, c):
        arrived = gathered(slot, c, every)
        values = [own[c, p] + arrived[p] for p in span]
        for p in span:
            out[slot, c, p] = values[p] * cell[0, p]
        return values

    def one_pair(pair, carry):
        for c in range(COMP):
            two_steps(arrive(2 * pair, c), 2 * pair + 1, c)
        ship_whole(2 * pair + 1)
        return carry

    lax.fori_loop(1, fine // 2 - 1, one_pair, 0)
    for c in range(COMP):
        two_steps(arrive(fine - 2, c), fine - 1, c, True)
    ship_whole(fine - 1)

    def finish(slot):
        await_whole(slot)
        for c in range(COMP):
            arrived = landed_sum(slot, c, near)
            for p in span:
                out[slot, c, p] = (out[slot, c, p] + arrived[p]) * cell[0, p]

    await_whole(0)
    for c in range(COMP):
        arrived = landed_sum(0, c, near)
        for p in span:
            base[c, p] = base[c, p] + arrived[p]

    def finish_pair(pair, carry):
        finish(2 * pair + 1)
        return carry

    lax.fori_loop(0, fine // 2 - 1, finish_pair, 0)

    last = tm == tms - 1
    odd = lax.rem(tm, 2) == 1
    inner = (1, 2, 3)

    def one_turn(state):
        return respond(state, {q: coarse_pull[q] * v for q, v in state.items()}, coarse_coef)

    def give(c, both):
        once = one_turn({mid + p: base[c, p] for p in span})
        turn_spread(once, 1, c, inner)
        if both:
            turn_spread(one_turn(once), 2, c, range(5))

    def take(phase, c, pieces):
        arrived = turn_gathered(phase, c, pieces)
        for p in span:
            base[c, p] = base[c, p] + arrived[p]

    for c in range(COMP):
        take(0, c, range(5))
        for p in span:
            base[c, p] = base[c, p] * cell[0, p] * cell[5, p]
        pl.when(jnp.logical_not(odd))(lambda c=c: give(c, False))
        pl.when(last)(lambda c=c: give(c, True))

    for c in range(COMP):
        take(1, c, inner)
        pl.when(odd)(lambda c=c: take(2, c, range(5)))
        pl.when(jnp.logical_and(odd, jnp.logical_not(last)))(lambda c=c: give(c, True))
        for p in span:
            out[0, c, p] = start[0, c, p] + base[c, p] * cell[3, p]
    finish(fine - 1)

    for at in every:

        @pl.when(reaches(SHIFTS[at]))
        def _():
            mat_copy(at).wait_send()

            def left(pair, carry):
                for c in range(COMP):
                    part_copy(2 * pair, at, c).wait_send()
                return carry

            lax.fori_loop(1, fine // 2, left, 0)
            if at in near:

                def left_whole(pair, carry):
                    whole_copy(2 * pair + 1, at).wait_send()
                    return carry

                lax.fori_loop(0, fine // 2, left_whole, 0)
                whole_copy(0, at).wait_send()

    def turns_left(phase, pieces):
        for piece in pieces:
            for c in range(COMP):
                with_piece(piece, lambda: turn_copy(phase, piece, c).wait_send())

    turns_left(0, range(5))
    turns_left(1, inner)
    pl.when(odd)(lambda: turns_left(2, range(5)))


def local(source, coarse_start, region, reluctivity, conductance):
    fine, comp, planes, rows, lanes = source.shape
    vmem = pl.BlockSpec(memory_space=pltpu.VMEM)
    hbm = pl.BlockSpec(memory_space=pltpu.HBM)
    slab = (planes, rows, lanes)
    return pl.pallas_call(
        functools.partial(kernel, lax.axis_size("tm"), lax.axis_size("space")),
        out_shape=jax.ShapeDtypeStruct(source.shape, source.dtype),
        in_specs=[hbm] * 5,
        out_specs=vmem,
        scratch_shapes=[
            pltpu.VMEM(source.shape, jnp.float32),
            pltpu.VMEM(coarse_start.shape, jnp.float32),
            pltpu.VMEM(region.shape, jnp.int32),
            pltpu.SMEM(reluctivity.shape, jnp.float32),
            pltpu.SMEM(conductance.shape, jnp.float32),
            pltpu.SemaphoreType.DMA((5,)),
            pltpu.VMEM((fine, 4, comp) + slab, jnp.float32),
            pltpu.VMEM((fine, 4, comp) + slab, jnp.float32),
            pltpu.VMEM((comp,) + slab, jnp.float32),
            pltpu.VMEM((comp,) + slab, jnp.float32),
            pltpu.VMEM((2,) + slab, jnp.float32),
            pltpu.VMEM((4, 2) + slab, jnp.float32),
            pltpu.VMEM((6, 5 * planes, rows, lanes), jnp.float32),
            pltpu.VMEM((6, 5 * planes, rows, lanes), jnp.float32),
            pltpu.VMEM((5 * planes, rows, lanes), jnp.float32),
            pltpu.VMEM((5 * planes, rows, lanes), jnp.float32),
            pltpu.VMEM((6,) + slab, jnp.float32),
            pltpu.VMEM((3, 5, comp) + slab, jnp.float32),
            pltpu.VMEM((3, 5, comp) + slab, jnp.float32),
            pltpu.SemaphoreType.DMA((4,)),
            pltpu.SemaphoreType.DMA((4,)),
            pltpu.SemaphoreType.DMA((fine, 4, comp)),
            pltpu.SemaphoreType.DMA((fine, 4, comp)),
            pltpu.SemaphoreType.DMA((3, 5, comp)),
            pltpu.SemaphoreType.DMA((3, 5, comp)),
        ],
        compiler_params=pltpu.CompilerParams(
            collective_id=0, has_side_effects=True, vmem_limit_bytes=32 * 1024 * 1024
        ),
        cost_estimate=pl.CostEstimate(
            flops=20_000_000, bytes_accessed=1_800_000, transcendentals=0
        ),
    )(source, coarse_start, region, reluctivity, conductance)


def solution(mesh):
    placed = (
        P("tm", None, "space", None, None),
        P("tm", None, "space", None, None),
        P("space", None, None),
        P(),
        P(),
    )
    return jax.shard_map(
        local,
        mesh=mesh,
        in_specs=placed,
        out_specs=P("tm", None, "space", None, None),
        check_vma=False,
    )
```

```python
import functools

import jax
import jax.numpy as jnp
from jax import lax
from jax.experimental import pallas as pl
from jax.experimental.pallas import tpu as pltpu
from jax.sharding import PartitionSpec as P

SWEEPS = 4
COMP = 3
LAMINATION = 8.0
SHIFTS = (-2, -1, 1, 2)
MESH = pl.DeviceIdType.MESH


def respond(first, drive, coef):
    current = first
    for _ in range(SWEEPS):
        if current is None:
            current = dict(drive)
            continue
        after = dict(drive)

        def add(plane, term):
            after[plane] = after[plane] + term if plane in after else term

        for q, value in current.items():
            add(q + 1, coef[0, q] * value)
            add(q - 1, coef[1, q] * value)
        for q, value in current.items():
            in_x = pltpu.roll(coef[2, q] * value, 1, 0) + pltpu.roll(coef[3, q] * value, 7, 0)
            in_y = pltpu.roll(coef[4, q] * value, 1, 1) + pltpu.roll(
                coef[5, q] * value, coef.shape[-1] - 1, 1
            )
            add(q, in_x + in_y)
        current = after
    return current


def kernel(
    tms,
    spaces,
    src_in,
    start_in,
    region_in,
    reluctivity_in,
    conductance_in,
    out,
    src,
    start,
    region,
    reluctivity,
    conductance,
    in_sem,
    sent,
    landed,
    own,
    base,
    mat_own,
    mat_far,
    fine_coef,
    coarse_coef,
    pull,
    coarse_pull,
    cell,
    turn_sent,
    turn_landed,
    mat_ssem,
    mat_rsem,
    ssem,
    rsem,
    turn_ssem,
    turn_rsem,
):
    fine, _, planes, rows, lanes = src.shape
    loads = [
        pltpu.make_async_copy(held, kept, in_sem.at[i])
        for i, (held, kept) in enumerate(
            (
                (reluctivity_in, reluctivity),
                (conductance_in, conductance),
                (region_in, region),
                (start_in, start),
                (src_in, src),
            )
        )
    ]
    for load in loads:
        load.start()
    tm = lax.axis_index("tm")
    me = lax.axis_index("space")
    after_tm = lax.rem(tm + 1, tms)
    before_tm = lax.rem(tm + tms - 1, tms)
    after_two = lax.rem(tm + 2, tms)
    before_two = lax.rem(tm + tms - 2, tms)
    mid = 2 * planes

    def reaches(shift):
        return me + shift >= 0 if shift < 0 else me + shift < spaces

    barrier = pltpu.get_barrier_semaphore()
    others = (after_tm, before_tm, after_two, before_two)
    for row in others:
        pl.semaphore_signal(barrier, inc=1, device_id=(row, me), device_id_type=MESH)
    neighbours = jnp.int32(4)
    for shift in SHIFTS:
        neighbours = neighbours + 5 * reaches(shift).astype(jnp.int32)

        @pl.when(reaches(shift))
        def _():
            for row in (tm,) + others:
                pl.semaphore_signal(barrier, inc=1, device_id=(row, me + shift), device_id_type=MESH)

    for load in loads[:3]:
        load.wait()
    for p in range(planes):
        kind = region[p]
        nu = jnp.zeros((rows, lanes), jnp.float32)
        s = jnp.zeros((rows, lanes), jnp.float32)
        for level in range(reluctivity.shape[0]):
            match = kind == level
            nu = jnp.where(match, reluctivity[level], nu)
            s = jnp.where(match, conductance[level], s)
        mat_own[0, p] = nu
        mat_own[1, p] = s

    zero = jnp.zeros((rows, lanes), jnp.float32)
    for at, shift in enumerate(SHIFTS):

        @pl.when(jnp.logical_not(reaches(shift)))
        def _():
            mat_far[at] = jnp.zeros(mat_far.shape[1:], jnp.float32)
            for phase in (0, 1, 2):
                turn_landed[phase, 2 + shift] = jnp.zeros(turn_landed.shape[2:], jnp.float32)

            def clear(slot, carry):
                landed[slot, at] = jnp.zeros(landed.shape[2:], jnp.float32)
                return carry

            lax.fori_loop(0, fine, clear, 0)

    pl.semaphore_wait(barrier, neighbours)

    def mat_copy(at, arrival=False):
        other = at if arrival else 3 - at
        return pltpu.make_async_remote_copy(
            src_ref=mat_own,
            dst_ref=mat_far.at[other],
            send_sem=mat_ssem.at[at],
            recv_sem=mat_rsem.at[other],
            device_id=(tm, me + SHIFTS[at]),
            device_id_type=MESH,
        )

    def whole_copy(slot, at, arrival=False):
        other = at if arrival else 3 - at
        return pltpu.make_async_remote_copy(
            src_ref=sent.at[slot, at],
            dst_ref=landed.at[slot, other],
            send_sem=ssem.at[slot, at, 0],
            recv_sem=rsem.at[slot, other, 0],
            device_id=(tm, me + SHIFTS[at]),
            device_id_type=MESH,
        )

    def part_copy(slot, at, c, arrival=False):
        other = at if arrival else 3 - at
        return pltpu.make_async_remote_copy(
            src_ref=sent.at[slot, at, c],
            dst_ref=landed.at[slot, other, c],
            send_sem=ssem.at[slot, at, c],
            recv_sem=rsem.at[slot, other, c],
            device_id=(tm, me + SHIFTS[at]),
            device_id_type=MESH,
        )

    def turn_copy(phase, piece, c, arrival=False):
        other = piece if arrival else 4 - piece
        return pltpu.make_async_remote_copy(
            src_ref=turn_sent.at[phase, piece, c],
            dst_ref=turn_landed.at[phase, other, c],
            send_sem=turn_ssem.at[phase, piece, c],
            recv_sem=turn_rsem.at[phase, other, c],
            device_id=(after_two if phase == 2 else after_tm, me + piece - 2),
            device_id_type=MESH,
        )

    def with_piece(piece, act):
        if piece == 2:
            act()
        else:
            pl.when(reaches(piece - 2))(act)

    for at in (1, 2, 0, 3):
        pl.when(reaches(SHIFTS[at]))(lambda at=at: mat_copy(at).start())
    for load in loads[3:]:
        load.wait()
    for at in (1, 2, 0, 3):
        pl.when(reaches(SHIFTS[at]))(lambda at=at: mat_copy(at, True).wait_recv())

    def whole(kind):
        gathered_planes = []
        for at in (0, 1, None, 2, 3):
            for p in range(planes):
                gathered_planes.append(mat_own[kind, p] if at is None else mat_far[at, kind, p])
        return gathered_planes

    nus, ss = whole(0), whole(1)
    row_at = lax.broadcasted_iota(jnp.int32, (rows, lanes), 0)
    lane_at = lax.broadcasted_iota(jnp.int32, (rows, lanes), 1)
    inside = []
    for shift in (-2, -1, 0, 1, 2):
        held = reaches(shift).astype(jnp.float32) if shift else jnp.float32(1.0)
        inside += [held] * planes
    for q in range(1, 5 * planes - 1):
        nu, s = nus[q], ss[q]
        up_z = (0.5 * LAMINATION) * (nus[q + 1] + nu)
        down_z = (0.5 * LAMINATION) * (nus[q - 1] + nu)
        up_x = 0.5 * (nu + jnp.where(row_at < rows - 1, pltpu.roll(nu, rows - 1, 0), 0.0))
        down_x = 0.5 * (nu + jnp.where(row_at > 0, pltpu.roll(nu, 1, 0), 0.0))
        up_y = 0.5 * (nu + jnp.where(lane_at < lanes - 1, pltpu.roll(nu, lanes - 1, 1), 0.0))
        down_y = 0.5 * (nu + jnp.where(lane_at > 0, pltpu.roll(nu, 1, 1), 0.0))
        summed = up_z + down_z + up_x + down_x + up_y + down_y
        gives = [
            up_z,
            down_z,
            jnp.where(row_at < rows - 1, up_x, 0.0),
            jnp.where(row_at > 0, down_x, 0.0),
            jnp.where(lane_at < lanes - 1, up_y, 0.0),
            jnp.where(lane_at > 0, down_y, 0.0),
        ]
        outside = 1.0 - inside[q]
        fine_d = s + summed
        coarse_d = s / fine + summed
        fine_inv = inside[q] / (fine_d + outside)
        coarse_inv = inside[q] / (coarse_d + outside)
        pull[q] = s * fine_inv
        coarse_pull[q] = s / fine * coarse_inv
        for which in range(6):
            fine_coef[which, q] = gives[which] * fine_inv
            coarse_coef[which, q] = gives[which] * coarse_inv
        if mid <= q < mid + planes:
            p = q - mid
            cell[0, p] = fine_inv
            cell[2, p] = fine_d
            cell[3, p] = coarse_inv
            cell[5, p] = coarse_d

    def store(reach, slot, at, c):
        begin = mid + SHIFTS[at] * planes
        for p in range(planes):
            sent[slot, at, c, p] = reach[begin + p] if begin + p in reach else zero

    def ship(slot, at, c):
        pl.when(reaches(SHIFTS[at]))(lambda: part_copy(slot, at, c).start())

    def ship_whole(slot):
        for at in near:
            pl.when(reaches(SHIFTS[at]))(lambda at=at: whole_copy(slot, at).start())

    def await_whole(slot):
        for at in near:
            pl.when(reaches(SHIFTS[at]))(lambda at=at: whole_copy(slot, at, True).wait_recv())

    def gathered(slot, c, sides):
        for at in sides:
            pl.when(reaches(SHIFTS[at]))(lambda at=at: part_copy(slot, at, c, True).wait_recv())
        return landed_sum(slot, c, sides)

    def landed_sum(slot, c, sides):
        total = []
        for p in range(planes):
            value = landed[slot, sides[0], c, p]
            for at in sides[1:]:
                value = value + landed[slot, at, c, p]
            total.append(value)
        return total

    def turn_spread(reach, phase, c, pieces):
        for piece in pieces:
            for p in range(planes):
                turn_sent[phase, piece, c, p] = reach[piece * planes + p]
        for piece in pieces:
            with_piece(piece, lambda piece=piece: turn_copy(phase, piece, c).start())

    def turn_gathered(phase, c, pieces):
        for piece in pieces:
            with_piece(piece, lambda piece=piece: turn_copy(phase, piece, c, True).wait_recv())
        total = []
        for p in range(planes):
            value = turn_landed[phase, pieces[0], c, p]
            for piece in pieces[1:]:
                value = value + turn_landed[phase, piece, c, p]
            total.append(value)
        return total

    near, every = (1, 2), (0, 1, 2, 3)
    span = range(planes)

    def fine_drive(state, slot, c):
        drive = {q: pull[q] * value for q, value in state.items()}
        if slot is not None:
            for p in span:
                drive[mid + p] = drive[mid + p] + src[slot, c, p]
        return drive

    def two_steps(values, slot, c, final=False):
        state = {mid + p: values[p] for p in span}
        halfway = respond(state, fine_drive(state, slot, c), fine_coef)
        reach = respond(
            halfway, fine_drive(halfway, None if final else slot + 1, c), fine_coef
        )
        for at in near:
            store(halfway, slot, at, c)
        if final:
            turn_spread(reach, 0, c, range(5))
        else:
            for at in every:
                store(reach, slot + 1, at, c)
            for at in every:
                ship(slot + 1, at, c)
            for p in span:
                own[c, p] = reach[mid + p]
        for p in span:
            out[slot, c, p] = halfway[mid + p]

    for c in range(COMP):
        two_steps([cell[2, p] * start[0, c, p] for p in span], 1, c)
    ship_whole(1)

    for c in range(COMP):
        reach = respond(None, {mid + p: src[0, c, p] for p in span}, fine_coef)
        for at in near:
            store(reach, 0, at, c)
        for p in span:
            base[c, p] = reach[mid + p] - cell[2, p] * start[0, c, p]
    ship_whole(0)

    def arrive(slot, c):
        arrived = gathered(slot, c, every)
        values = [own[c, p] + arrived[p] for p in span]
        for p in span:
            out[slot, c, p] = values[p] * cell[0, p]
        return values

    def one_pair(pair, carry):
        for c in range(COMP):
            two_steps(arrive(2 * pair, c), 2 * pair + 1, c)
        ship_whole(2 * pair + 1)
        return carry

    lax.fori_loop(1, fine // 2 - 1, one_pair, 0)
    for c in range(COMP):
        two_steps(arrive(fine - 2, c), fine - 1, c, True)
    ship_whole(fine - 1)

    def finish(slot):
        await_whole(slot)
        for c in range(COMP):
            arrived = landed_sum(slot, c, near)
            for p in span:
                out[slot, c, p] = (out[slot, c, p] + arrived[p]) * cell[0, p]

    await_whole(0)
    for c in range(COMP):
        arrived = landed_sum(0, c, near)
        for p in span:
            base[c, p] = base[c, p] + arrived[p]

    def finish_pair(pair, carry):
        finish(2 * pair + 1)
        return carry

    lax.fori_loop(0, fine // 2 - 1, finish_pair, 0)

    for at in every:

        @pl.when(reaches(SHIFTS[at]))
        def _():
            mat_copy(at).wait_send()

            def left(pair, carry):
                for c in range(COMP):
                    part_copy(2 * pair, at, c).wait_send()
                return carry

            lax.fori_loop(1, fine // 2, left, 0)
            if at in near:

                def left_whole(pair, carry):
                    whole_copy(2 * pair + 1, at).wait_send()
                    return carry

                lax.fori_loop(0, fine // 2 - 1, left_whole, 0)
                whole_copy(0, at).wait_send()

    last = tm == tms - 1
    odd = lax.rem(tm, 2) == 1
    inner = (1, 2, 3)

    def one_turn(state):
        return respond(state, {q: coarse_pull[q] * v for q, v in state.items()}, coarse_coef)

    def give(c, both):
        once = one_turn({mid + p: base[c, p] for p in span})
        turn_spread(once, 1, c, inner)
        if both:
            turn_spread(one_turn(once), 2, c, range(5))

    def take(phase, c, pieces):
        arrived = turn_gathered(phase, c, pieces)
        for p in span:
            base[c, p] = base[c, p] + arrived[p]

    for c in range(COMP):
        take(0, c, range(5))
        for p in span:
            base[c, p] = base[c, p] * cell[0, p] * cell[5, p]
        pl.when(jnp.logical_not(odd))(lambda c=c: give(c, False))
        pl.when(last)(lambda c=c: give(c, True))

    for c in range(COMP):
        take(1, c, inner)
        pl.when(odd)(lambda c=c: take(2, c, range(5)))
        pl.when(jnp.logical_and(odd, jnp.logical_not(last)))(lambda c=c: give(c, True))
        for p in span:
            out[0, c, p] = start[0, c, p] + base[c, p] * cell[3, p]
    finish(fine - 1)

    for at in near:
        pl.when(reaches(SHIFTS[at]))(lambda at=at: whole_copy(fine - 1, at).wait_send())

    def turns_left(phase, pieces):
        for piece in pieces:
            for c in range(COMP):
                with_piece(piece, lambda: turn_copy(phase, piece, c).wait_send())

    turns_left(0, range(5))
    turns_left(1, inner)
    pl.when(odd)(lambda: turns_left(2, range(5)))


def local(source, coarse_start, region, reluctivity, conductance):
    fine, comp, planes, rows, lanes = source.shape
    vmem = pl.BlockSpec(memory_space=pltpu.VMEM)
    hbm = pl.BlockSpec(memory_space=pltpu.HBM)
    slab = (planes, rows, lanes)
    return pl.pallas_call(
        functools.partial(kernel, lax.axis_size("tm"), lax.axis_size("space")),
        out_shape=jax.ShapeDtypeStruct(source.shape, source.dtype),
        in_specs=[hbm] * 5,
        out_specs=vmem,
        scratch_shapes=[
            pltpu.VMEM(source.shape, jnp.float32),
            pltpu.VMEM(coarse_start.shape, jnp.float32),
            pltpu.VMEM(region.shape, jnp.int32),
            pltpu.SMEM(reluctivity.shape, jnp.float32),
            pltpu.SMEM(conductance.shape, jnp.float32),
            pltpu.SemaphoreType.DMA((5,)),
            pltpu.VMEM((fine, 4, comp) + slab, jnp.float32),
            pltpu.VMEM((fine, 4, comp) + slab, jnp.float32),
            pltpu.VMEM((comp,) + slab, jnp.float32),
            pltpu.VMEM((comp,) + slab, jnp.float32),
            pltpu.VMEM((2,) + slab, jnp.float32),
            pltpu.VMEM((4, 2) + slab, jnp.float32),
            pltpu.VMEM((6, 5 * planes, rows, lanes), jnp.float32),
            pltpu.VMEM((6, 5 * planes, rows, lanes), jnp.float32),
            pltpu.VMEM((5 * planes, rows, lanes), jnp.float32),
            pltpu.VMEM((5 * planes, rows, lanes), jnp.float32),
            pltpu.VMEM((6,) + slab, jnp.float32),
            pltpu.VMEM((3, 5, comp) + slab, jnp.float32),
            pltpu.VMEM((3, 5, comp) + slab, jnp.float32),
            pltpu.SemaphoreType.DMA((4,)),
            pltpu.SemaphoreType.DMA((4,)),
            pltpu.SemaphoreType.DMA((fine, 4, comp)),
            pltpu.SemaphoreType.DMA((fine, 4, comp)),
            pltpu.SemaphoreType.DMA((3, 5, comp)),
            pltpu.SemaphoreType.DMA((3, 5, comp)),
        ],
        compiler_params=pltpu.CompilerParams(
            collective_id=0, has_side_effects=True, vmem_limit_bytes=32 * 1024 * 1024
        ),
        cost_estimate=pl.CostEstimate(
            flops=20_000_000, bytes_accessed=1_800_000, transcendentals=0
        ),
    )(source, coarse_start, region, reluctivity, conductance)


def solution(mesh):
    placed = (
        P("tm", None, "space", None, None),
        P("tm", None, "space", None, None),
        P("space", None, None),
        P(),
        P(),
    )
    return jax.shard_map(
        local,
        mesh=mesh,
        in_specs=placed,
        out_specs=P("tm", None, "space", None, None),
        check_vma=False,
    )
```
